32 devices in a mesh: rad: 16 (over z, y, x), col: 2 (over core).
Axes of the slice: x: 2, y: 2, z: 4, core: 2. Of those that a mesh axis runs over, the one named last changes fastest.
Arguments:
- right_sides: bfloat16 [64, 384, 1024], P('rad', None, 'col'), may hold values from -6 to 6
- coarse_solution: bfloat16 [16, 384, 1024], P('rad', None, 'col'), may hold values from -6 to 6
- lift_one: bfloat16 [32, 2, 1024, 1024], P('rad', None, 'col'), may hold values from -0.125 to 0.125
- solve_one: bfloat16 [32, 3, 1024, 1024], P('rad', None, 'col'), may hold values from -0.109375 to 0.109375
- lift_two: bfloat16 [16, 2, 1024, 1024], P('rad', None, 'col'), may hold values from -0.125 to 0.125
- solve_two: bfloat16 [16, 3, 1024, 1024], P('rad', None, 'col'), may hold values from -0.109375 to 0.109375
Outputs:
- solution: bfloat16 [64, 384, 1024], P('rad', None, 'col')
- reduced_sides: bfloat16 [16, 384, 1024], P('rad', None, 'col')
The draws below stay inside these ranges and needn't reach their ends.
All inputs are finite; a program needn't handle non-finite values.
Results may differ from the reference program's by a relative error of at most 0.007.
Values may be sent and summed in bfloat16 or wider, within the bound.
A program may use at most 64 MiB of HBM per device.

```python
import jax
import jax.numpy as jnp
from jax import lax

CHANNELS = 1024
VECTORS = 384
BLOCKS = 64
GROUPS = 16


def level_of(rng, extent, shards, least, high):
    def one(axis_at, blocks):
        heights = jax.random.uniform(jax.random.fold_in(jax.random.fold_in(rng, 6), axis_at), (blocks,), jnp.float32, least / len(shards), high / len(shards))
        return jnp.repeat(jnp.exp(heights), extent[axis_at] // blocks).reshape((-1,) + (1,) * (len(extent) - axis_at - 1))

    factor_of = one(*shards[0])
    for cut in shards[1:]:
        factor_of = factor_of * one(*cut)
    return factor_of


def centred(stream_key, dims, spread, most, split=(), held_as=jnp.bfloat16):
    drawn = jax.random.normal(stream_key, dims, jnp.float32) * spread
    if len(split) > 0:
        drawn = level_of(stream_key, dims, split, -0.22, 0.18) * drawn
    return jnp.clip(drawn, min=-most, max=most).astype(held_as)


def setup_inputs(seed: int = 0) -> dict:
    seeds = jax.random.split(jax.random.key(seed), 7)
    return {
        "right_sides": centred(seeds[0], (BLOCKS, VECTORS, CHANNELS), 1.0, 6.0, ((0, 16), (2, 2))),
        "coarse_solution": centred(seeds[1], (GROUPS, VECTORS, CHANNELS), 1.0, 6.0, ((0, 16), (2, 2))),
        "lift_one": centred(seeds[2], (BLOCKS // 2, 2, CHANNELS, CHANNELS), (2 * CHANNELS) ** -0.5, 0.125, ((0, 16), (2, 2))),
        "solve_one": centred(seeds[3], (BLOCKS // 2, 3, CHANNELS, CHANNELS), (3 * CHANNELS) ** -0.5, 0.109375, ((0, 16), (2, 2))),
        "lift_two": centred(seeds[4], (GROUPS, 2, CHANNELS, CHANNELS), (2 * CHANNELS) ** -0.5, 0.125, ((0, 16), (2, 2))),
        "solve_two": centred(seeds[5], (GROUPS, 3, CHANNELS, CHANNELS), (3 * CHANNELS) ** -0.5, 0.109375, ((0, 16), (2, 2))),
    }


def apply(vector, matrix):
    return jnp.dot(vector, matrix.T, preferred_element_type=jnp.float32)


def level_one(inputs):
    quartet, before, lift = inputs
    first = quartet[0].astype(jnp.float32) - apply(before, lift[0, 0]) - apply(quartet[1], lift[0, 1])
    third = quartet[2].astype(jnp.float32) - apply(quartet[1], lift[1, 0]) - apply(quartet[3], lift[1, 1])
    return first.astype(jnp.bfloat16), third.astype(jnp.bfloat16)


def level_two(inputs):
    kept, middle, middle_before, quartet, lift_pair, solve_pair, solve_triple, coarse_here, coarse_next = inputs
    reduced = kept.astype(jnp.float32) - apply(middle_before, lift_pair[0]) - apply(middle, lift_pair[1])
    centre = apply(middle, solve_triple[0]) - apply(coarse_here, solve_triple[1]) - apply(coarse_next, solve_triple[2])
    centre = centre.astype(jnp.bfloat16)
    second = apply(quartet[1], solve_pair[0, 0]) - apply(coarse_here, solve_pair[0, 1]) - apply(centre, solve_pair[0, 2])
    fourth = apply(quartet[3], solve_pair[1, 0]) - apply(centre, solve_pair[1, 1]) - apply(coarse_next, solve_pair[1, 2])
    stacked = jnp.stack([coarse_here, second.astype(jnp.bfloat16), centre, fourth.astype(jnp.bfloat16)])
    return reduced.astype(jnp.bfloat16), stacked


def reference(right_sides, coarse_solution, lift_one, solve_one, lift_two, solve_two):
    groups = BLOCKS // 4
    quartets = right_sides.reshape(groups, 4, VECTORS, CHANNELS)
    zero_block = jnp.zeros((1, VECTORS, CHANNELS), right_sides.dtype)
    before = jnp.concatenate([zero_block, quartets[:-1, 3]], axis=0)
    after = jnp.concatenate([coarse_solution[1:], zero_block], axis=0)
    lift_groups = lift_one.reshape(groups, 2, 2, CHANNELS, CHANNELS)
    kept, middle = lax.map(level_one, (quartets, before, lift_groups))
    middle_before = jnp.concatenate([zero_block, middle[:-1]], axis=0)
    solve_groups = solve_one.reshape(groups, 2, 3, CHANNELS, CHANNELS)
    reduced, solved = lax.map(level_two, (kept, middle, middle_before, quartets, lift_two, solve_groups, solve_two, coarse_solution, after))
    return solved.reshape(BLOCKS, VECTORS, CHANNELS), reduced
```

```python
import functools

import jax
import jax.numpy as jnp
from jax import lax
from jax.experimental import pallas as pl
from jax.experimental.pallas import tpu as pltpu
from jax.sharding import PartitionSpec as P

MESH = pl.DeviceIdType.MESH
F32 = jnp.float32
BF16 = jnp.bfloat16

B1, B3, COARSE, BEFORE, NEXT, MID, MIDBEF, CENTRE = range(8)
KEPT, RED, CEN, SEC, FOU = range(5)
L1, S1, L2, S2 = range(4)
WEIGHTS = (
    (L1, 1, 0), (L1, 1, 1), (L1, 0, 1), (S1, 0, 0), (S1, 1, 0), (S1, 0, 1), (S2, 0, 1), (S2, 0, 0),
    (L2, 0, 1), (S2, 0, 2), (S1, 1, 2), (S1, 0, 2), (S1, 1, 1), (L1, 0, 0), (L2, 0, 0),
)
SLOT = {w: i for i, w in enumerate(WEIGHTS)}


def kernel(R, C, NQ, rs, co, l1, s1, l2, s2, sol, red,
           full, wv, own, acc, stage, wsem, lsem, osem, csend, crecv, rsend, rrecv):
    V, D = rs.shape[1], rs.shape[2]
    Q = V // NQ
    TN = min(256, D)
    r = lax.axis_index("rad")
    c = lax.axis_index("col")
    has_up, has_down = r < R - 1, r > 0
    mats = (l1, s1, l2, s2)

    def load(i):
        m, a, b = WEIGHTS[i]
        return pltpu.make_async_copy(mats[m].at[a, b], wv.at[i], wsem.at[i])

    locals_ = (
        pltpu.make_async_copy(rs.at[1], full.at[B1, c], lsem.at[0]),
        pltpu.make_async_copy(rs.at[3], full.at[B3, c], lsem.at[1]),
        pltpu.make_async_copy(co.at[0], full.at[COARSE, c], lsem.at[2]),
        pltpu.make_async_copy(rs.at[2], own.at[1], lsem.at[3]),
        pltpu.make_async_copy(rs.at[0], own.at[0], lsem.at[4]),
    )
    keep = pltpu.make_async_copy(co.at[0], sol.at[0], osem.at[0])

    def across(tag, slot, rows, src):
        out = []
        for d in range(1, C):
            peer = lax.rem(c + d, C)
            out.append(pltpu.make_async_remote_copy(
                src_ref=src,
                dst_ref=full.at[tag, c, rows],
                send_sem=csend.at[slot, d - 1],
                recv_sem=crecv.at[slot, d - 1],
                device_id={"col": peer},
                device_id_type=MESH,
            ))
        return out

    def arrived(tag, slot, rows):
        for d in range(1, C):
            peer = lax.rem(c + C - d, C)
            pltpu.make_async_remote_copy(
                src_ref=full.at[tag, peer, rows],
                dst_ref=full.at[tag, peer, rows],
                send_sem=csend.at[slot, d - 1],
                recv_sem=crecv.at[slot, d - 1],
                device_id={"col": peer},
                device_id_type=MESH,
            ).wait_recv()

    every = pl.ds(0, V)

    def part(q):
        return pl.ds(q * Q, Q)

    def along(kind, q):
        tag = (NEXT, BEFORE, MIDBEF)[kind]
        src = (co.at[0, part(q)], rs.at[3, part(q)], full.at[MID, c, part(q)])[kind]
        return pltpu.make_async_remote_copy(
            src_ref=src,
            dst_ref=full.at[tag, c, part(q)],
            send_sem=rsend.at[kind, q],
            recv_sem=rrecv.at[kind, q],
            device_id={"rad": r - 1 if kind == 0 else r + 1},
            device_id_type=MESH,
        )

    def slot_of(tag, q=0):
        if tag in (B1, B3, COARSE, MID, CENTRE):
            return (B1, B3, COARSE, MID, CENTRE).index(tag)
        return 5 + (NEXT, BEFORE, MIDBEF).index(tag) * NQ + q

    locals_[0].start()
    locals_[1].start()
    load(0).start()
    load(1).start()
    locals_[3].start()

    barrier = pltpu.get_barrier_semaphore()
    for d in range(1, C):
        pl.semaphore_signal(barrier, inc=1, device_id={"col": lax.rem(c + d, C)}, device_id_type=MESH)

    @pl.when(has_up)
    def _():
        pl.semaphore_signal(barrier, inc=1, device_id={"rad": r + 1}, device_id_type=MESH)

    @pl.when(has_down)
    def _():
        pl.semaphore_signal(barrier, inc=1, device_id={"rad": r - 1}, device_id_type=MESH)

    pl.semaphore_wait(barrier, C - 1 + has_up.astype(jnp.int32) + has_down.astype(jnp.int32))

    sent = []

    def share(tag, slot, rows, src):
        for copy in across(tag, slot, rows, src):
            copy.start()
            sent.append(copy)

    @pl.when(has_down)
    def _():
        for q in range(NQ):
            along(0, q).start()

    share(B1, slot_of(B1), every, rs.at[1])
    share(B3, slot_of(B3), every, rs.at[3])

    @pl.when(has_up)
    def _():
        for q in range(NQ):
            along(1, q).start()

    share(COARSE, slot_of(COARSE), every, co.at[0])
    locals_[2].start()
    locals_[4].start()
    for i in range(2, len(WEIGHTS)):
        load(i).start()
    keep.start()

    @pl.when(r == 0)
    def _():
        full[BEFORE] = jnp.zeros_like(full[BEFORE])
        full[MIDBEF] = jnp.zeros_like(full[MIDBEF])

    @pl.when(r == R - 1)
    def _():
        full[NEXT] = jnp.zeros_like(full[NEXT])

    def times(tag, weight, rows, columns):
        i = SLOT[weight]
        total = None
        for s in range(C):
            term = lax.dot_general(
                full[tag, s, rows, :], wv[i, columns, s * D:(s + 1) * D],
                (((1,), (1,)), ((), ())), preferred_element_type=F32,
            )
            total = term if total is None else total + term
        return total

    def tiles(body):
        @pl.loop(0, D // TN)
        def _(t):
            body(pl.ds(pl.multiple_of(t * TN, TN), TN))

    def ready(*weights):
        for w in weights:
            load(SLOT[w]).wait()

    locals_[0].wait()
    locals_[1].wait()
    locals_[3].wait()
    ready((L1, 1, 0), (L1, 1, 1))
    arrived(B1, slot_of(B1), every)
    arrived(B3, slot_of(B3), every)

    def mid(n):
        full[MID, c, :, n] = (
            own[1, :, n].astype(F32) - times(B1, (L1, 1, 0), every, n) - times(B3, (L1, 1, 1), every, n)
        ).astype(BF16)

    tiles(mid)
    share(MID, slot_of(MID), every, full.at[MID, c])

    @pl.when(has_up)
    def _():
        for q in range(NQ):
            along(2, q).start()

    locals_[4].wait()
    ready((L1, 0, 1), (S1, 0, 0), (S1, 1, 0))

    def first(n):
        acc[KEPT, :, n] = own[0, :, n].astype(F32) - times(B1, (L1, 0, 1), every, n)
        acc[FOU, :, n] = times(B3, (S1, 1, 0), every, n)

    tiles(first)
    locals_[2].wait()
    arrived(COARSE, slot_of(COARSE), every)
    ready((S1, 0, 1), (S2, 0, 1))

    def with_coarse(n):
        acc[SEC, :, n] = times(B1, (S1, 0, 0), every, n) - times(COARSE, (S1, 0, 1), every, n)

    tiles(with_coarse)
    arrived(MID, slot_of(MID), every)
    ready((S2, 0, 0), (L2, 0, 1))

    def with_mid(n):
        acc[CEN, :, n] = times(MID, (S2, 0, 0), every, n) - times(COARSE, (S2, 0, 1), every, n)
        acc[RED, :, n] = times(MID, (L2, 0, 1), every, n)

    tiles(with_mid)

    def relay(kind, tag, there, q):
        @pl.when(there)
        def _():
            along(kind, q).wait_recv()
            for copy in across(tag, slot_of(tag, q), part(q), full.at[tag, c, part(q)]):
                copy.start()

    def relayed(tag, there, q):
        @pl.when(there)
        def _():
            arrived(tag, slot_of(tag, q), part(q))

    for q in range(NQ):
        relay(0, NEXT, has_up, q)
    ready((S2, 0, 2), (S1, 1, 2))
    for q in range(NQ):
        relayed(NEXT, has_up, q)

    def centre(n):
        full[CENTRE, c, :, n] = (acc[CEN, :, n] - times(NEXT, (S2, 0, 2), every, n)).astype(BF16)

    tiles(centre)
    share(CENTRE, slot_of(CENTRE), every, full.at[CENTRE, c])
    centre_out = pltpu.make_async_copy(full.at[CENTRE, c], sol.at[2], osem.at[1])
    centre_out.start()

    def with_next(n):
        acc[FOU, :, n] = acc[FOU, :, n] - times(NEXT, (S1, 1, 2), every, n)

    tiles(with_next)
    ready((S1, 0, 2), (S1, 1, 1))
    arrived(CENTRE, slot_of(CENTRE), every)

    def odd(n):
        stage[0, :, n] = (acc[SEC, :, n] - times(CENTRE, (S1, 0, 2), every, n)).astype(BF16)
        stage[1, :, n] = (acc[FOU, :, n] - times(CENTRE, (S1, 1, 1), every, n)).astype(BF16)

    tiles(odd)
    second_out = pltpu.make_async_copy(stage.at[0], sol.at[1], osem.at[2])
    fourth_out = pltpu.make_async_copy(stage.at[1], sol.at[3], osem.at[3])
    second_out.start()
    fourth_out.start()

    for q in range(NQ):
        relay(1, BEFORE, has_down, q)
    ready((L1, 0, 0))
    for q in range(NQ):
        relayed(BEFORE, has_down, q)

    def kept(n):
        whole = (acc[KEPT, :, n] - times(BEFORE, (L1, 0, 0), every, n)).astype(BF16)
        acc[RED, :, n] = whole.astype(F32) - acc[RED, :, n]

    tiles(kept)

    ready((L2, 0, 0))
    reds = [pltpu.make_async_copy(stage.at[2, part(q)], red.at[0, part(q)], osem.at[4 + q]) for q in range(NQ)]

    def last(q):
        relayed(MIDBEF, has_down, q)

        def body(n):
            stage[2, part(q), n] = (
                acc[RED, part(q), n] - times(MIDBEF, (L2, 0, 0), part(q), n)
            ).astype(BF16)

        tiles(body)
        reds[q].start()

    for q in range(NQ):
        relay(2, MIDBEF, has_down, q)
        if q > 0:
            last(q - 1)
    last(NQ - 1)

    for copy in sent:
        copy.wait_send()

    @pl.when(has_down)
    def _():
        for q in range(NQ):
            along(0, q).wait_send()
            for tag in (BEFORE, MIDBEF):
                for copy in across(tag, slot_of(tag, q), part(q), full.at[tag, c, part(q)]):
                    copy.wait_send()

    @pl.when(has_up)
    def _():
        for q in range(NQ):
            along(1, q).wait_send()
            along(2, q).wait_send()
            for copy in across(NEXT, slot_of(NEXT, q), part(q), full.at[NEXT, c, part(q)]):
                copy.wait_send()

    keep.wait()
    centre_out.wait()
    second_out.wait()
    fourth_out.wait()
    for copy in reds:
        copy.wait()


def local(R, C, right_sides, coarse_solution, lift_one, solve_one, lift_two, solve_two):
    _, V, D = right_sides.shape
    K = lift_one.shape[-1]
    NQ = 4 if V % 64 == 0 else 1
    peers = max(C - 1, 1)
    moved = sum(a.size for a in (right_sides, coarse_solution, lift_one, solve_one, lift_two, solve_two))
    any_ = pl.BlockSpec(memory_space=pl.ANY)
    return pl.pallas_call(
        functools.partial(kernel, R, C, NQ),
        out_shape=(
            jax.ShapeDtypeStruct(right_sides.shape, BF16),
            jax.ShapeDtypeStruct(coarse_solution.shape, BF16),
        ),
        in_specs=[any_] * 6,
        out_specs=(any_, any_),
        scratch_shapes=[
            pltpu.VMEM((8, C, V, D), BF16),
            pltpu.VMEM((len(WEIGHTS), D, K), BF16),
            pltpu.VMEM((2, V, D), BF16),
            pltpu.VMEM((5, V, D), F32),
            pltpu.VMEM((3, V, D), BF16),
            pltpu.SemaphoreType.DMA((len(WEIGHTS),)),
            pltpu.SemaphoreType.DMA((5,)),
            pltpu.SemaphoreType.DMA((4 + NQ,)),
            pltpu.SemaphoreType.DMA((5 + 3 * NQ, peers)),
            pltpu.SemaphoreType.DMA((5 + 3 * NQ, peers)),
            pltpu.SemaphoreType.DMA((3, NQ)),
            pltpu.SemaphoreType.DMA((3, NQ)),
        ],
        compiler_params=pltpu.CompilerParams(
            collective_id=0, has_side_effects=True, vmem_limit_bytes=48 * 1024 * 1024
        ),
        cost_estimate=pl.CostEstimate(
            flops=2 * len(WEIGHTS) * V * D * K, bytes_accessed=4 * moved, transcendentals=0
        ),
    )(right_sides, coarse_solution, lift_one, solve_one, lift_two, solve_two)


def solution(mesh):
    return jax.shard_map(
        functools.partial(local, mesh.shape["rad"], mesh.shape["col"]),
        mesh=mesh,
        in_specs=(
            P("rad", None, "col"),
            P("rad", None, "col"),
            P("rad", None, "col", None),
            P("rad", None, "col", None),
            P("rad", None, "col", None),
            P("rad", None, "col", None),
        ),
        out_specs=(P("rad", None, "col"), P("rad", None, "col")),
        check_vma=False,
    )
```

```python
import functools

import jax
import jax.numpy as jnp
from jax import lax
from jax.experimental import pallas as pl
from jax.experimental.pallas import tpu as pltpu
from jax.sharding import PartitionSpec as P

MESH = pl.DeviceIdType.MESH
F32 = jnp.float32
BF16 = jnp.bfloat16

B1, B3, COARSE, BEFORE, NEXT, MID, MIDBEF, CENTRE = range(8)
KEPT, RED, CEN, SEC, FOU = range(5)
L1, S1, L2, S2 = range(4)
WEIGHTS = (
    (L1, 1, 0), (L1, 1, 1), (L1, 0, 1), (S1, 0, 0), (S1, 1, 0), (S1, 0, 1), (S2, 0, 1), (S2, 0, 0),
    (L2, 0, 1), (S2, 0, 2), (S1, 1, 2), (S1, 0, 2), (S1, 1, 1), (L1, 0, 0), (L2, 0, 0),
)
SLOT = {w: i for i, w in enumerate(WEIGHTS)}


def kernel(R, C, NQ, rs, co, l1, s1, l2, s2, sol, red,
           full, wv, own, acc, stage, wsem, lsem, osem, csend, crecv, rsend, rrecv):
    V, D = rs.shape[1], rs.shape[2]
    Q = V // NQ
    TN = min(256, D)
    r = lax.axis_index("rad")
    c = lax.axis_index("col")
    has_up, has_down = r < R - 1, r > 0
    mats = (l1, s1, l2, s2)

    def load(i):
        m, a, b = WEIGHTS[i]
        return pltpu.make_async_copy(mats[m].at[a, b], wv.at[i], wsem.at[i])

    locals_ = (
        pltpu.make_async_copy(rs.at[1], full.at[B1, c], lsem.at[0]),
        pltpu.make_async_copy(rs.at[3], full.at[B3, c], lsem.at[1]),
        pltpu.make_async_copy(co.at[0], full.at[COARSE, c], lsem.at[2]),
        pltpu.make_async_copy(rs.at[2], own.at[1], lsem.at[3]),
        pltpu.make_async_copy(rs.at[0], own.at[0], lsem.at[4]),
    )
    keep = pltpu.make_async_copy(co.at[0], sol.at[0], osem.at[0])

    def across(tag, slot, rows, src):
        out = []
        for d in range(1, C):
            peer = lax.rem(c + d, C)
            out.append(pltpu.make_async_remote_copy(
                src_ref=src,
                dst_ref=full.at[tag, c, rows],
                send_sem=csend.at[slot, d - 1],
                recv_sem=crecv.at[slot, d - 1],
                device_id={"col": peer},
                device_id_type=MESH,
            ))
        return out

    def arrived(tag, slot, rows):
        for d in range(1, C):
            peer = lax.rem(c + C - d, C)
            pltpu.make_async_remote_copy(
                src_ref=full.at[tag, peer, rows],
                dst_ref=full.at[tag, peer, rows],
                send_sem=csend.at[slot, d - 1],
                recv_sem=crecv.at[slot, d - 1],
                device_id={"col": peer},
                device_id_type=MESH,
            ).wait_recv()

    every = pl.ds(0, V)

    def part(q):
        return pl.ds(q * Q, Q)

    def along(kind, q):
        tag = (NEXT, BEFORE, MIDBEF)[kind]
        src = (co.at[0, part(q)], rs.at[3, part(q)], full.at[MID, c, part(q)])[kind]
        return pltpu.make_async_remote_copy(
            src_ref=src,
            dst_ref=full.at[tag, c, part(q)],
            send_sem=rsend.at[kind, q],
            recv_sem=rrecv.at[kind, q],
            device_id={"rad": r - 1 if kind == 0 else r + 1},
            device_id_type=MESH,
        )

    def slot_of(tag, q=0):
        if tag in (B1, B3, COARSE, MID, CENTRE):
            return (B1, B3, COARSE, MID, CENTRE).index(tag)
        return 5 + (NEXT, BEFORE, MIDBEF).index(tag) * NQ + q

    locals_[0].start()
    locals_[1].start()
    load(0).start()
    load(1).start()
    locals_[3].start()

    barrier = pltpu.get_barrier_semaphore()
    for d in range(1, C):
        pl.semaphore_signal(barrier, inc=1, device_id={"col": lax.rem(c + d, C)}, device_id_type=MESH)

    @pl.when(has_up)
    def _():
        pl.semaphore_signal(barrier, inc=1, device_id={"rad": r + 1}, device_id_type=MESH)

    @pl.when(has_down)
    def _():
        pl.semaphore_signal(barrier, inc=1, device_id={"rad": r - 1}, device_id_type=MESH)

    pl.semaphore_wait(barrier, C - 1 + has_up.astype(jnp.int32) + has_down.astype(jnp.int32))

    sent = []

    def share(tag, slot, rows, src):
        for copy in across(tag, slot, rows, src):
            copy.start()
            sent.append(copy)

    @pl.when(has_down)
    def _():
        for q in range(NQ):
            along(0, q).start()

    share(B1, slot_of(B1), every, rs.at[1])
    share(B3, slot_of(B3), every, rs.at[3])

    share(COARSE, slot_of(COARSE), every, co.at[0])
    locals_[2].start()
    locals_[4].start()
    for i in range(2, len(WEIGHTS)):
        load(i).start()
    keep.start()

    @pl.when(r == 0)
    def _():
        full[BEFORE] = jnp.zeros_like(full[BEFORE])
        full[MIDBEF] = jnp.zeros_like(full[MIDBEF])

    @pl.when(r == R - 1)
    def _():
        full[NEXT] = jnp.zeros_like(full[NEXT])

    def times(tag, weight, rows, columns):
        i = SLOT[weight]
        total = None
        for s in range(C):
            term = lax.dot_general(
                full[tag, s, rows, :], wv[i, columns, s * D:(s + 1) * D],
                (((1,), (1,)), ((), ())), preferred_element_type=F32,
            )
            total = term if total is None else total + term
        return total

    def tiles(body):
        @pl.loop(0, D // TN)
        def _(t):
            body(pl.ds(pl.multiple_of(t * TN, TN), TN))

    def ready(*weights):
        for w in weights:
            load(SLOT[w]).wait()

    locals_[0].wait()
    locals_[1].wait()
    locals_[3].wait()
    ready((L1, 1, 0), (L1, 1, 1))
    arrived(B1, slot_of(B1), every)
    arrived(B3, slot_of(B3), every)

    def mid(n):
        full[MID, c, :, n] = (
            own[1, :, n].astype(F32) - times(B1, (L1, 1, 0), every, n) - times(B3, (L1, 1, 1), every, n)
        ).astype(BF16)

    tiles(mid)
    share(MID, slot_of(MID), every, full.at[MID, c])

    locals_[4].wait()
    ready((L1, 0, 1), (S1, 0, 0), (S1, 1, 0))

    def first(n):
        acc[KEPT, :, n] = own[0, :, n].astype(F32) - times(B1, (L1, 0, 1), every, n)
        acc[FOU, :, n] = times(B3, (S1, 1, 0), every, n)

    tiles(first)
    locals_[2].wait()
    arrived(COARSE, slot_of(COARSE), every)
    ready((S1, 0, 1), (S2, 0, 1))

    def with_coarse(n):
        acc[SEC, :, n] = times(B1, (S1, 0, 0), every, n) - times(COARSE, (S1, 0, 1), every, n)

    tiles(with_coarse)
    arrived(MID, slot_of(MID), every)
    ready((S2, 0, 0), (L2, 0, 1))

    def with_mid(n):
        acc[CEN, :, n] = times(MID, (S2, 0, 0), every, n) - times(COARSE, (S2, 0, 1), every, n)
        acc[RED, :, n] = times(MID, (L2, 0, 1), every, n)

    tiles(with_mid)


    def relay(kind, tag, there, q):
        @pl.when(there)
        def _():
            along(kind, q).wait_recv()
            for copy in across(tag, slot_of(tag, q), part(q), full.at[tag, c, part(q)]):
                copy.start()

    def relayed(tag, there, q):
        @pl.when(there)
        def _():
            arrived(tag, slot_of(tag, q), part(q))

    for q in range(NQ):
        relay(0, NEXT, has_up, q)
    @pl.when(has_down)
    def _():
        for q in range(NQ):
            along(0, q).wait_send()

    @pl.when(has_up)
    def _():
        for q in range(NQ):
            along(1, q).start()
        for q in range(NQ):
            along(2, q).start()

    ready((S2, 0, 2), (S1, 1, 2))
    for q in range(NQ):
        relayed(NEXT, has_up, q)

    def centre(n):
        full[CENTRE, c, :, n] = (acc[CEN, :, n] - times(NEXT, (S2, 0, 2), every, n)).astype(BF16)

    tiles(centre)
    share(CENTRE, slot_of(CENTRE), every, full.at[CENTRE, c])
    centre_out = pltpu.make_async_copy(full.at[CENTRE, c], sol.at[2], osem.at[1])
    centre_out.start()

    def with_next(n):
        acc[FOU, :, n] = acc[FOU, :, n] - times(NEXT, (S1, 1, 2), every, n)

    tiles(with_next)
    ready((S1, 0, 2), (S1, 1, 1))
    arrived(CENTRE, slot_of(CENTRE), every)

    def odd(n):
        stage[0, :, n] = (acc[SEC, :, n] - times(CENTRE, (S1, 0, 2), every, n)).astype(BF16)
        stage[1, :, n] = (acc[FOU, :, n] - times(CENTRE, (S1, 1, 1), every, n)).astype(BF16)

    tiles(odd)
    second_out = pltpu.make_async_copy(stage.at[0], sol.at[1], osem.at[2])
    fourth_out = pltpu.make_async_copy(stage.at[1], sol.at[3], osem.at[3])
    second_out.start()
    fourth_out.start()


    for q in range(NQ):
        relay(1, BEFORE, has_down, q)
    ready((L1, 0, 0))
    for q in range(NQ):
        relayed(BEFORE, has_down, q)

    def kept(n):
        whole = (acc[KEPT, :, n] - times(BEFORE, (L1, 0, 0), every, n)).astype(BF16)
        acc[RED, :, n] = whole.astype(F32) - acc[RED, :, n]

    tiles(kept)

    ready((L2, 0, 0))
    reds = [pltpu.make_async_copy(stage.at[2, part(q)], red.at[0, part(q)], osem.at[4 + q]) for q in range(NQ)]

    def last(q):
        relayed(MIDBEF, has_down, q)

        def body(n):
            stage[2, part(q), n] = (
                acc[RED, part(q), n] - times(MIDBEF, (L2, 0, 0), part(q), n)
            ).astype(BF16)

        tiles(body)
        reds[q].start()

    for q in range(NQ):
        relay(2, MIDBEF, has_down, q)
        if q > 0:
            last(q - 1)
    last(NQ - 1)

    for copy in sent:
        copy.wait_send()

    @pl.when(has_down)
    def _():
        for q in range(NQ):
            for tag in (BEFORE, MIDBEF):
                for copy in across(tag, slot_of(tag, q), part(q), full.at[tag, c, part(q)]):
                    copy.wait_send()

    @pl.when(has_up)
    def _():
        for q in range(NQ):
            along(1, q).wait_send()
            along(2, q).wait_send()
            for copy in across(NEXT, slot_of(NEXT, q), part(q), full.at[NEXT, c, part(q)]):
                copy.wait_send()

    keep.wait()
    centre_out.wait()
    second_out.wait()
    fourth_out.wait()
    for copy in reds:
        copy.wait()


def local(R, C, right_sides, coarse_solution, lift_one, solve_one, lift_two, solve_two):
    _, V, D = right_sides.shape
    K = lift_one.shape[-1]
    NQ = 4 if V % 64 == 0 else 1
    peers = max(C - 1, 1)
    moved = sum(a.size for a in (right_sides, coarse_solution, lift_one, solve_one, lift_two, solve_two))
    any_ = pl.BlockSpec(memory_space=pl.ANY)
    return pl.pallas_call(
        functools.partial(kernel, R, C, NQ),
        out_shape=(
            jax.ShapeDtypeStruct(right_sides.shape, BF16),
            jax.ShapeDtypeStruct(coarse_solution.shape, BF16),
        ),
        in_specs=[pl.BlockSpec(memory_space=pltpu.HBM)] * 6,
        out_specs=(any_, any_),
        scratch_shapes=[
            pltpu.VMEM((8, C, V, D), BF16),
            pltpu.VMEM((len(WEIGHTS), D, K), BF16),
            pltpu.VMEM((2, V, D), BF16),
            pltpu.VMEM((5, V, D), F32),
            pltpu.VMEM((3, V, D), BF16),
            pltpu.SemaphoreType.DMA((len(WEIGHTS),)),
            pltpu.SemaphoreType.DMA((5,)),
            pltpu.SemaphoreType.DMA((4 + NQ,)),
            pltpu.SemaphoreType.DMA((5 + 3 * NQ, peers)),
            pltpu.SemaphoreType.DMA((5 + 3 * NQ, peers)),
            pltpu.SemaphoreType.DMA((3, NQ)),
            pltpu.SemaphoreType.DMA((3, NQ)),
        ],
        compiler_params=pltpu.CompilerParams(
            collective_id=0, has_side_effects=True, vmem_limit_bytes=60 * 1024 * 1024
        ),
        cost_estimate=pl.CostEstimate(
            flops=2 * len(WEIGHTS) * V * D * K, bytes_accessed=4 * moved, transcendentals=0
        ),
    )(right_sides, coarse_solution, lift_one, solve_one, lift_two, solve_two)


def solution(mesh):
    return jax.shard_map(
        functools.partial(local, mesh.shape["rad"], mesh.shape["col"]),
        mesh=mesh,
        in_specs=(
            P("rad", None, "col"),
            P("rad", None, "col"),
            P("rad", None, "col", None),
            P("rad", None, "col", None),
            P("rad", None, "col", None),
            P("rad", None, "col", None),
        ),
        out_specs=(P("rad", None, "col"), P("rad", None, "col")),
        check_vma=False,
    )
```
